256 devices in a mesh: rows: 32 (over x, y, core), height: 8 (over z).
Axes of the slice: x: 4, y: 4, z: 8, core: 2. Of those that a mesh axis runs over, the one named last changes fastest.
Arguments:
- snapshots: float32 [64, 256, 128, 128], P(None, 'rows', 'height'), may hold values from -200 to 200
- material: int32 [256, 128, 128], P('rows', 'height'), may hold values from 0 to 2
Outputs:
- basis: float32 [64, 256, 128, 128], P(None, 'rows', 'height')
- applied: float32 [64, 256, 128, 128], P(None, 'rows', 'height')
- reduced: float32 [64, 64], replicated
- low_factor: float32 [64, 64], replicated
The draws below stay inside these ranges and needn't reach their ends.
All inputs are finite; a program needn't handle non-finite values.
Results may differ from the reference program's by a relative error of at most 0.00014.
Values sent between devices are 32-bit elements; how exact they have to be, the bound alone decides.
A program may use at most 64 MiB of HBM per device.

```python
import jax
import jax.numpy as jnp
from jax import lax

M = 64
NY = 128
NX = 256
NZ = 128
NCELLS = 4194304


def draw_snapshots(key, part):
    key = jax.random.fold_in(key, 11)
    key_rough = jax.random.fold_in(key, 1)
    ramp_x = jnp.arange(NX, dtype=jnp.float32)[:, None, None] / NX
    ramp_z = jnp.arange(NZ, dtype=jnp.float32)[None, :, None] / NZ
    envelope = (1.0 + 2.0 * ramp_x) * (1.0 + 0.5 * ramp_z)
    values = jnp.clip(jax.random.normal(key_rough, (M, NX, NZ, NY), jnp.float32), -6.0, 6.0)
    return (envelope * values).astype(jnp.float32)


def touch_ends(values, key, low, largest):
    longest = values.shape.index(max(values.shape))
    spots = []
    for shift in (0, 1):
        where = [jax.random.randint(jax.random.fold_in(key, axis), (), 0, length) for axis, length in enumerate(values.shape)]
        where[longest] = (where[longest] + shift) % values.shape[longest]
        spots.append(tuple(where))
    return values.at[spots[0]].set(low).at[spots[1]].set(largest)


def setup_inputs(seed: int = 0) -> dict:
    splits = jax.random.split(jax.random.key(seed), 3)
    return {
        "snapshots": draw_snapshots(jax.random.fold_in(splits[2], 71), 0),
        "material": touch_ends(jax.random.randint(splits[1], (NX, NZ, NY), 0, 3), jax.random.fold_in(splits[1], 1), 0, 2).astype(jnp.int32),
    }


CONDUCT_TABLE = (0.5, 2.0, 1.0)
COUPLE_TABLE = (0.3, 0.1, 0.6)

def lookup(material, table):
    return jnp.where(material == 0, table[0], jnp.where(material == 1, table[1], table[2])).astype(jnp.float32)

def neighbour(padded_in, axis_pos, offset):
    leading = padded_in.ndim - 3
    pieces = []
    for position in range(3):
        extent = padded_in.shape[leading + position]
        if position == axis_pos:
            pieces.append(slice(1 + offset, extent - 1 + offset))
        else:
            pieces.append(slice(1, extent - 1))
    return padded_in[(slice(None),) * leading + tuple(pieces)]

def apply_stencil(field_pad, conduct_pad, conduct, coupling):
    center = field_pad[:, 1:-1, 1:-1, 1:-1]
    result = coupling * center
    for axis_pos in range(3):
        for offset in (-1, 1):
            beside = neighbour(field_pad, axis_pos, offset)
            link = 0.5 * (conduct + neighbour(conduct_pad, axis_pos, offset))
            result = result + link * (center - beside)
    return result

def reference(snapshots, material):
    conduct = lookup(material, CONDUCT_TABLE)
    coupling = lookup(material, COUPLE_TABLE)
    conduct_pad = jnp.pad(conduct, 1)
    flat = snapshots.reshape(M, -1)
    gram = jnp.dot(flat, flat.T, precision=lax.Precision.HIGHEST) / NCELLS
    low_factor = jnp.linalg.cholesky(gram)
    basis_flat = jax.scipy.linalg.solve_triangular(low_factor, flat, lower=True)
    basis = basis_flat.reshape(snapshots.shape)

    def one_column(column):
        padded = jnp.pad(column, 1)[None]
        return apply_stencil(padded, conduct_pad, conduct, coupling)[0]
    applied = lax.map(one_column, basis)
    reduced = jnp.dot(basis_flat, applied.reshape(M, -1).T, precision=lax.Precision.HIGHEST) / NCELLS
    return (basis, applied, reduced, low_factor)
```

```python
import functools

import jax
import jax.numpy as jnp
from jax import lax
from jax.experimental import pallas as pl
from jax.experimental.pallas import tpu as pltpu
from jax.sharding import PartitionSpec as P

CONDUCT_TABLE = (0.5, 2.0, 1.0)
COUPLE_TABLE = (0.3, 0.1, 0.6)
MESH = pl.DeviceIdType.MESH
F32 = jnp.float32
BF16 = jnp.bfloat16
M = 64
NXL, NZL, NY = 8, 16, 128
LANES = NZL * NY
ROWS, HEIGHT = 32, 8
CELLS = 4194304


def lookup(material, table):
    return jnp.where(material == 0, table[0], jnp.where(material == 1, table[1], table[2])).astype(F32)


def split3(f):
    h = f.astype(BF16)
    r = f - h.astype(F32)
    m = r.astype(BF16)
    return h, m, (r - m.astype(F32)).astype(BF16)


def tree_sum(vals):
    while len(vals) > 1:
        vals = [vals[i] + vals[i + 1] if i + 1 < len(vals) else vals[i] for i in range(0, len(vals), 2)]
    return vals[0]


def zsl(z):
    return slice(z * NY, (z + 1) * NY)


def pack(g):
    return jnp.concatenate([g[0:32], g[32:64]], axis=1)


def unpack(g):
    return jnp.concatenate([g[:, 0:64], g[:, 64:128]], axis=0)


def nt_dot(a, b):
    return lax.dot_general(a, b, (((1,), (1,)), ((), ())), preferred_element_type=F32)


def first_kernel(
    snap, mat_in, f3, i3, w_out, pt_out,
    mat, fld, hz_lo, hz_hi, cond, faces, coef, acc, acc2,
    mine, from_c, xy_buf, z_buf, half, whole,
    load_sem, fx_send, fx_recv, ar_send, ar_recv,
):
    r = lax.axis_index("rows")
    z = lax.axis_index("height")
    xy, c = r // 2, r % 2
    up_r, dn_r = (r + 1) % ROWS, (r + ROWS - 1) % ROWS
    up_z, dn_z = (z + 1) % HEIGHT, (z + HEIGHT - 1) % HEIGHT
    partner = (xy * 2 + (1 - c), z)

    def remote(src, dst, ss, rs, dev):
        return pltpu.make_async_remote_copy(
            src_ref=src, dst_ref=dst, send_sem=ss, recv_sem=rs, device_id=dev, device_id_type=MESH
        )

    def drain(ref, sem):
        pltpu.make_async_copy(ref, ref, sem).wait()

    def load(x):
        for zz in range(NZL):
            pltpu.make_async_copy(
                snap.at[:, x, zz, :], fld.at[x + 1, :, zsl(zz)], load_sem.at[x]
            ).start()

    def load_body(i, carry):
        load(i)
        return carry

    pltpu.make_async_copy(mat_in, mat, load_sem.at[NXL]).start()
    load(0)
    load(NXL - 1)
    lax.fori_loop(1, NXL - 1, load_body, 0)

    bar = pltpu.get_barrier_semaphore()

    def greet(dev):
        pl.semaphore_signal(bar, inc=1, device_id=dev, device_id_type=MESH)

    greet((up_r, z))
    greet((dn_r, z))
    greet(partner)
    for k in range(1, 16):
        greet((((xy + k) % 16) * 2 + c, z))
    for k in range(1, HEIGHT):
        greet((r, (z + k) % HEIGHT))

    drain(mat, load_sem.at[NXL])
    cond[...] = lookup(mat[...], CONDUCT_TABLE)
    faces[0] = cond[NXL - 1]
    faces[1] = cond[0]
    faces[2, 0:8] = cond[:, NZL - 1, :]
    faces[3, 0:8] = cond[:, 0, :]
    acc[...] = jnp.zeros_like(acc)
    acc2[...] = jnp.zeros_like(acc2)

    pl.semaphore_wait(bar, 2 + 1 + 15 + 7)
    remote(faces.at[0], faces.at[4], fx_send.at[0], fx_recv.at[0], (up_r, z)).start()
    remote(faces.at[1], faces.at[5], fx_send.at[1], fx_recv.at[1], (dn_r, z)).start()
    remote(faces.at[2, 0:8], faces.at[6, 0:8], fx_send.at[2], fx_recv.at[2], (r, up_z)).start()
    remote(faces.at[3, 0:8], faces.at[7, 0:8], fx_send.at[3], fx_recv.at[3], (r, dn_z)).start()

    def gram_part(x):
        drain(fld.at[x + 1], load_sem.at[x])
        remote(fld.at[x + 1, :, zsl(NZL - 1)], hz_lo.at[x], fx_send.at[4], fx_recv.at[4], (r, up_z)).start()
        remote(fld.at[x + 1, :, zsl(0)], hz_hi.at[x], fx_send.at[5], fx_recv.at[5], (r, dn_z)).start()
        for zz in range(NZL):
            h, m, low = split3(fld[x + 1, :, zsl(zz)])
            f3[x, 0:64, zsl(zz)] = h
            f3[x, 64:128, zsl(zz)] = m
            f3[x, 128:192, zsl(zz)] = low
        acc[...] += nt_dot(f3[x, 0:128], f3[x])

    gram_part(0)
    remote(fld.at[1], fld.at[NXL + 1], fx_send.at[6], fx_recv.at[6], (dn_r, z)).start()
    gram_part(NXL - 1)
    remote(fld.at[NXL], fld.at[0], fx_send.at[7], fx_recv.at[7], (up_r, z)).start()

    def gram_body(x, carry):
        gram_part(x)
        return carry

    lax.fori_loop(1, NXL - 1, gram_body, 0)

    def sum_start(i, value):
        mine[i] = value
        remote(
            mine.at[i, pl.ds(pl.multiple_of((1 - c) * 16, 16), 16)], from_c.at[i],
            ar_send.at[4 * i], ar_recv.at[4 * i], partner,
        ).start()

    def sum_xy(i):
        drain(from_c.at[i], ar_recv.at[4 * i])
        half[i, 0] = mine[i, pl.ds(pl.multiple_of(c * 16, 16), 16), :] + from_c[i]
        for k in range(1, 16):
            remote(
                half.at[i, 0], xy_buf.at[i, xy], ar_send.at[4 * i + 1], ar_recv.at[4 * i + 1],
                (((xy + k) % 16) * 2 + c, z),
            ).start()
        xy_buf[i, xy] = half[i, 0]

    def sum_z(i):
        drain(xy_buf.at[i, 0:15], ar_recv.at[4 * i + 1])
        half[i, 1] = tree_sum([xy_buf[i, k] for k in range(16)])
        for k in range(1, HEIGHT):
            remote(
                half.at[i, 1], z_buf.at[i, z], ar_send.at[4 * i + 2], ar_recv.at[4 * i + 2],
                (r, (z + k) % HEIGHT),
            ).start()
        z_buf[i, z] = half[i, 1]

    def sum_c(i):
        drain(z_buf.at[i, 0:7], ar_recv.at[4 * i + 2])
        here = whole.at[i, pl.ds(pl.multiple_of(c * 16, 16), 16)]
        here[...] = tree_sum([z_buf[i, k] for k in range(HEIGHT)])
        remote(here, here, ar_send.at[4 * i + 3], ar_recv.at[4 * i + 3], partner).start()

    def sum_end(i):
        there = whole.at[i, pl.ds(pl.multiple_of((1 - c) * 16, 16), 16)]
        drain(there, ar_recv.at[4 * i + 3])
        return unpack(whole[i])

    a = acc[...]
    cross = a[0:64, 64:128] + a[0:64, 128:192]
    gram = (a[0:64, 0:64] + (cross + cross.T) + a[64:128, 64:128]) * (1.0 / CELLS)
    sum_start(0, pack(gram))
    sum_xy(0)

    for i in range(4):
        drain(faces.at[4 + i] if i < 2 else faces.at[4 + i, 0:8], fx_recv.at[i])
    row_id = lax.broadcasted_iota(jnp.int32, (NZL, NY), 0)
    lane_id = lax.broadcasted_iota(jnp.int32, (NZL, NY), 1)
    ok_lo_x = jnp.where(r > 0, 1.0, 0.0).astype(F32)
    ok_hi_x = jnp.where(r < ROWS - 1, 1.0, 0.0).astype(F32)
    ok_lo_z = jnp.where(z > 0, 1.0, 0.0).astype(F32)
    ok_hi_z = jnp.where(z < HEIGHT - 1, 1.0, 0.0).astype(F32)
    for x in range(NXL):
        cc = cond[x]
        couple = lookup(mat[x], COUPLE_TABLE)
        half_c = 0.5 * cc
        diag = couple
        if x == 0:
            lo = 0.5 * (cc + faces[4]) * ok_lo_x
            diag = diag + half_c * (1.0 - ok_lo_x)
        else:
            lo = 0.5 * (cc + cond[x - 1])
        if x == NXL - 1:
            hi = 0.5 * (cc + faces[5]) * ok_hi_x
            diag = diag + half_c * (1.0 - ok_hi_x)
        else:
            hi = 0.5 * (cc + cond[x + 1])
        below = jnp.concatenate([faces[6, x : x + 1], cc[0 : NZL - 1]], axis=0)
        above = jnp.concatenate([cc[1:NZL], faces[7, x : x + 1]], axis=0)
        mask_lo = jnp.where(row_id == 0, ok_lo_z, 1.0)
        mask_hi = jnp.where(row_id == NZL - 1, ok_hi_z, 1.0)
        zlo = 0.5 * (cc + below) * mask_lo
        zhi = 0.5 * (cc + above) * mask_hi
        diag = diag + half_c * ((1.0 - mask_lo) + (1.0 - mask_hi))
        nxt = pltpu.roll(cc, NY - 1, 1)
        ly = jnp.where(lane_id == NY - 1, 0.0, 0.5 * (cc + nxt))
        edge = jnp.where((lane_id == 0) | (lane_id == NY - 1), half_c, 0.0)
        coef[0, x] = diag + edge
        coef[1, x] = lo
        coef[2, x] = hi
        coef[3, x] = zlo
        coef[4, x] = zhi
        coef[5, x] = ly

    drain(hz_lo, fx_recv.at[4])
    drain(hz_hi, fx_recv.at[5])
    drain(fld.at[NXL + 1], fx_recv.at[6])
    drain(fld.at[0], fx_recv.at[7])

    def image_part(x, carry):
        for zz in range(NZL):
            v = fld[x + 1, :, zsl(zz)]

            def cf(i):
                return coef[i, x, zz : zz + 1, :]

            out = cf(0) * v
            out += cf(1) * (v - fld[x, :, zsl(zz)])
            out += cf(2) * (v - fld[x + 2, :, zsl(zz)])
            out += cf(3) * (v - (hz_lo[x] if zz == 0 else fld[x + 1, :, zsl(zz - 1)]))
            out += cf(4) * (v - (hz_hi[x] if zz == NZL - 1 else fld[x + 1, :, zsl(zz + 1)]))
            q = cf(5) * (v - pltpu.roll(v, NY - 1, 1))
            out += q - pltpu.roll(q, 1, 1)
            h, m, low = split3(out)
            i3[x, 0:64, zsl(zz)] = h
            i3[x, 64:128, zsl(zz)] = m
            i3[x, 128:192, zsl(zz)] = low
        acc2[...] += nt_dot(f3[x], i3[x])
        return carry

    lax.fori_loop(0, NXL, image_part, 0)
    sum_z(0)

    a = acc2[...]
    proj = (
        a[0:64, 0:64]
        + (a[0:64, 64:128] + a[64:128, 0:64])
        + (a[0:64, 128:192] + a[64:128, 64:128] + a[128:192, 0:64])
    ) * (1.0 / CELLS)
    sum_start(1, pack(proj))
    sum_xy(1)
    sum_c(0)
    g = sum_end(0)
    sum_z(1)

    ri = lax.broadcasted_iota(jnp.int32, (M, M), 0)
    ci = lax.broadcasted_iota(jnp.int32, (M, M), 1)
    rows = lax.broadcasted_iota(jnp.int32, (M, 2 * M), 0)
    w = jnp.concatenate([g, jnp.where(ri == ci, 1.0, 0.0).astype(F32)], axis=1)
    for j in range(M - 1):
        row = w[j : j + 1, :]
        mult = w[:, j : j + 1] * (1.0 / w[j : j + 1, j : j + 1])
        w = jnp.where(rows > j, w - mult * row, w)
    w_out[...] = w

    sum_c(1)
    pt_out[...] = sum_end(1)

    for i in range(4):
        drain(faces.at[4] if i < 2 else faces.at[4, 0:8], fx_send.at[i])
    drain(hz_lo, fx_send.at[4])
    drain(hz_hi, fx_send.at[5])
    drain(fld.at[0], fx_send.at[6])
    drain(fld.at[0], fx_send.at[7])
    for i in range(2):
        drain(from_c.at[i], ar_send.at[4 * i])
        drain(xy_buf.at[i, 0:15], ar_send.at[4 * i + 1])
        drain(z_buf.at[i, 0:7], ar_send.at[4 * i + 2])
        drain(from_c.at[i], ar_send.at[4 * i + 3])


def last_kernel(f3, i3, w_in, pt, basis, applied, reduced, low_factor, st, lst, sem):
    w = w_in[...]
    ri = lax.broadcasted_iota(jnp.int32, (M, M), 0)
    ci = lax.broadcasted_iota(jnp.int32, (M, M), 1)
    u = w[:, 0:M]
    d = jnp.sum(jnp.where(ri == ci, u, 0.0), axis=1, keepdims=True)
    rs = lax.rsqrt(d)
    linv = jnp.where(ci <= ri, w[:, M : 2 * M] * rs, 0.0)
    h, m, low = split3(linv)
    zero = jnp.zeros_like(h)
    lst[...] = jnp.concatenate(
        [
            jnp.concatenate([h, h, h], axis=1),
            jnp.concatenate([m, m, zero], axis=1),
            jnp.concatenate([low, zero, zero], axis=1),
        ],
        axis=0,
    )

    def part(x, carry):
        for i, (src, dst) in enumerate(((f3, basis), (i3, applied))):
            for col in range(0, LANES, 512):
                p = jnp.dot(lst[...], src[x, :, col : col + 512], preferred_element_type=F32)
                st[i, x, :, col : col + 512] = p[0:64] + (p[64:128] + p[128:192])
            for zz in range(NZL):
                pltpu.make_async_copy(st.at[i, x, :, zsl(zz)], dst.at[:, x, zz, :], sem).start()
        return carry

    lax.fori_loop(0, NXL, part, 0)
    low_factor[...] = jnp.where(ci >= ri, u * rs, 0.0).T
    hi = lax.Precision.HIGHEST
    t = jnp.dot(linv, pt[...], precision=hi, preferred_element_type=F32)
    reduced[...] = lax.dot_general(
        t, linv, (((1,), (1,)), ((), ())), precision=hi, preferred_element_type=F32
    )
    pltpu.make_async_copy(st, st, sem).wait()


def local(snapshots, material):
    any_ = pl.BlockSpec(memory_space=pl.ANY)
    vm = pl.BlockSpec(memory_space=pltpu.VMEM)
    dma, fbuf = pltpu.SemaphoreType.DMA, functools.partial(pltpu.VMEM, dtype=F32)
    wide = pltpu.VMEM((NXL, 192, LANES), BF16)
    f3, i3, w, pt = pl.pallas_call(
        first_kernel,
        out_shape=(
            wide,
            wide,
            jax.ShapeDtypeStruct((M, 2 * M), F32),
            jax.ShapeDtypeStruct((M, M), F32),
        ),
        in_specs=[any_, any_],
        out_specs=(vm, vm, vm, vm),
        scratch_shapes=[
            pltpu.VMEM((NXL, NZL, NY), jnp.int32),
            fbuf((NXL + 2, M, LANES)),
            fbuf((NXL, M, NY)),
            fbuf((NXL, M, NY)),
            fbuf((NXL, NZL, NY)),
            fbuf((8, NZL, NY)),
            fbuf((6, NXL, NZL, NY)),
            fbuf((128, 192)),
            fbuf((192, 192)),
            fbuf((2, 32, 128)),
            fbuf((2, 16, 128)),
            fbuf((2, 16, 16, 128)),
            fbuf((2, 8, 16, 128)),
            fbuf((2, 2, 16, 128)),
            fbuf((2, 32, 128)),
            dma((NXL + 1,)),
            dma((8,)),
            dma((8,)),
            dma((8,)),
            dma((8,)),
        ],
        compiler_params=pltpu.CompilerParams(
            collective_id=0, has_side_effects=True, vmem_limit_bytes=24 << 20
        ),
        name="gram_and_image",
    )(
        pltpu.with_memory_space_constraint(snapshots, pltpu.HBM),
        pltpu.with_memory_space_constraint(material, pltpu.HBM),
    )
    full = jax.ShapeDtypeStruct((M, NXL, NZL, NY), F32)
    small = jax.ShapeDtypeStruct((M, M), F32)
    return pl.pallas_call(
        last_kernel,
        out_shape=(full, full, small, small),
        in_specs=[vm, vm, vm, vm],
        out_specs=(any_, any_, vm, vm),
        scratch_shapes=[fbuf((2, NXL, M, LANES)), pltpu.VMEM((192, 192), BF16), dma],
        compiler_params=pltpu.CompilerParams(vmem_limit_bytes=24 << 20),
        name="apply_inverse",
    )(f3, i3, w, pt)


def solution(mesh):
    in_specs = (P(None, "rows", "height", None), P("rows", "height", None))
    out_specs = (P(None, "rows", "height", None), P(None, "rows", "height", None), P(), P())
    return jax.shard_map(local, mesh=mesh, in_specs=in_specs, out_specs=out_specs, check_vma=False)
```

```python
import functools

import jax
import jax.numpy as jnp
from jax import lax
from jax.experimental import pallas as pl
from jax.experimental.pallas import tpu as pltpu
from jax.sharding import PartitionSpec as P

CONDUCT_TABLE = (0.5, 2.0, 1.0)
COUPLE_TABLE = (0.3, 0.1, 0.6)
MESH = pl.DeviceIdType.MESH
F32 = jnp.float32
BF16 = jnp.bfloat16
M = 64
NXL, NZL, NY = 8, 16, 128
LANES = NZL * NY
ROWS, HEIGHT = 32, 8
CELLS = 4194304
PARTS = (slice(0, 64),)


def lookup(material, table):
    return jnp.where(material == 0, table[0], jnp.where(material == 1, table[1], table[2])).astype(F32)


def split3(f):
    h = f.astype(BF16)
    r = f - h.astype(F32)
    m = r.astype(BF16)
    return h, m, (r - m.astype(F32)).astype(BF16)


def tree_sum(vals):
    while len(vals) > 1:
        vals = [vals[i] + vals[i + 1] if i + 1 < len(vals) else vals[i] for i in range(0, len(vals), 2)]
    return vals[0]


def zsl(z):
    return slice(z * NY, (z + 1) * NY)


def pack(g):
    return jnp.concatenate([g[0:32], g[32:64]], axis=1)


def unpack(g):
    return jnp.concatenate([g[:, 0:64], g[:, 64:128]], axis=0)


def nt_dot(a, b):
    return lax.dot_general(a, b, (((1,), (1,)), ((), ())), preferred_element_type=F32)


def eliminate(w):
    blocks = [w[8 * k : 8 * k + 8] for k in range(8)]
    rid = lax.broadcasted_iota(jnp.int32, (8, 2 * M), 0)

    def over_lanes(v, j):
        return jnp.broadcast_to(v[:, j : j + 1], (8, 2 * M))

    def over_rows(v, s):
        return jnp.broadcast_to(v[s : s + 1, :], (8, 2 * M))

    for b in range(8):
        full = upper = blocks[b]
        cols = [over_lanes(full, 8 * b + s) for s in range(8)]
        below = [[over_lanes(blocks[k], 8 * b + s) for s in range(8)] for k in range(b + 1, 8)]
        for s in range(8):
            inv = 1.0 / over_rows(cols[s], s)
            here = rid == s
            mult = cols[s] * inv
            upper = jnp.where(here, full, upper)
            full = jnp.where(here, full * inv, full - mult * over_rows(full, s))
            for t in range(s + 1, 8):
                cols[t] = jnp.where(here, cols[t] * inv, cols[t] - mult * over_rows(cols[t], s))
        rows = [over_rows(full, s) for s in range(8)]
        for k in range(b + 1, 8):
            blocks[k] = blocks[k] - tree_sum([below[k - b - 1][s] * rows[s] for s in range(8)])
        blocks[b] = upper
    return jnp.concatenate(blocks, axis=0)


def first_kernel(
    snap, mat_in, basis_v, applied_v, w_out, pt_out,
    mat, fld, lay, f3, i3, hz_out, hz_lo, hz_hi, cond, faces, coef, acc, acc2,
    mine, from_c, xy_buf, z_buf, half, whole, lst,
    load_sem, fx_send, fx_recv, ar_send, ar_recv,
):
    r = lax.axis_index("rows")
    z = lax.axis_index("height")
    xy, c = r // 2, r % 2
    up_r, dn_r = (r + 1) % ROWS, (r + ROWS - 1) % ROWS
    up_z, dn_z = (z + 1) % HEIGHT, (z + HEIGHT - 1) % HEIGHT
    partner = (xy * 2 + (1 - c), z)

    def remote(src, dst, ss, rs, dev):
        return pltpu.make_async_remote_copy(
            src_ref=src, dst_ref=dst, send_sem=ss, recv_sem=rs, device_id=dev, device_id_type=MESH
        )

    def drain(ref, sem):
        pltpu.make_async_copy(ref, ref, sem).wait()

    def slab(x, zz):
        return fld.at[x].reshape(M * NZL, NY)[pl.ds(zz, M, stride=NZL), :]

    pltpu.make_async_copy(mat_in, mat, load_sem.at[NXL]).start()
    for x in (0, NXL - 1, *range(1, NXL - 1)):
        pltpu.make_async_copy(snap.at[:, x], fld.at[x], load_sem.at[x]).start()

    bar = pltpu.get_barrier_semaphore()

    def greet(dev):
        pl.semaphore_signal(bar, inc=1, device_id=dev, device_id_type=MESH)

    greet((up_r, z))
    greet((dn_r, z))
    greet(partner)
    for k in range(1, 16):
        greet((((xy + k) % 16) * 2 + c, z))
    for k in range(1, HEIGHT):
        greet((r, (z + k) % HEIGHT))

    drain(mat, load_sem.at[NXL])
    cond[...] = lookup(mat[...], CONDUCT_TABLE)
    faces[0] = cond[NXL - 1]
    faces[1] = cond[0]
    faces[2, 0:8] = cond[:, NZL - 1, :]
    faces[3, 0:8] = cond[:, 0, :]
    acc[...] = jnp.zeros_like(acc)
    acc2[...] = jnp.zeros_like(acc2)

    def gram_part(x):
        for zz in range(NZL):
            v = slab(x, zz)
            lay[x + 1, :, zsl(zz)] = v
            if zz == 0:
                hz_out[0, x] = v
            if zz == NZL - 1:
                hz_out[1, x] = v
            h, m, low = split3(v)
            f3[x, 0:64, zsl(zz)] = h
            f3[x, 64:128, zsl(zz)] = m
            f3[x, 128:192, zsl(zz)] = low
        acc[...] += nt_dot(f3[x, 0:128], f3[x])

    def send_z(x):
        remote(hz_out.at[1, x], hz_lo.at[x], fx_send.at[4], fx_recv.at[4], (r, up_z)).start()
        remote(hz_out.at[0, x], hz_hi.at[x], fx_send.at[5], fx_recv.at[5], (r, dn_z)).start()

    drain(fld.at[0], load_sem.at[0])
    gram_part(0)
    drain(fld.at[NXL - 1], load_sem.at[NXL - 1])

    pl.semaphore_wait(bar, 2 + 1 + 15 + 7)
    remote(faces.at[0], faces.at[4], fx_send.at[0], fx_recv.at[0], (up_r, z)).start()
    remote(faces.at[1], faces.at[5], fx_send.at[1], fx_recv.at[1], (dn_r, z)).start()
    remote(faces.at[2, 0:8], faces.at[6, 0:8], fx_send.at[2], fx_recv.at[2], (r, up_z)).start()
    remote(faces.at[3, 0:8], faces.at[7, 0:8], fx_send.at[3], fx_recv.at[3], (r, dn_z)).start()
    remote(lay.at[1], lay.at[NXL + 1], fx_send.at[6], fx_recv.at[6], (dn_r, z)).start()
    send_z(0)
    gram_part(NXL - 1)
    remote(lay.at[NXL], lay.at[0], fx_send.at[7], fx_recv.at[7], (up_r, z)).start()
    send_z(NXL - 1)

    def gram_body(x, carry):
        drain(fld.at[x], load_sem.at[x])
        gram_part(x)
        send_z(x)
        return carry

    lax.fori_loop(1, NXL - 1, gram_body, 0)

    def sum_start(i, value):
        mine[i] = value
        remote(
            mine.at[i, pl.ds(pl.multiple_of((1 - c) * 16, 16), 16)], from_c.at[i],
            ar_send.at[4 * i], ar_recv.at[4 * i], partner,
        ).start()

    def sum_xy(i):
        drain(from_c.at[i], ar_recv.at[4 * i])
        half[i, 0] = mine[i, pl.ds(pl.multiple_of(c * 16, 16), 16), :] + from_c[i]
        for k in range(1, 16):
            remote(
                half.at[i, 0], xy_buf.at[i, xy], ar_send.at[4 * i + 1], ar_recv.at[4 * i + 1],
                (((xy + k) % 16) * 2 + c, z),
            ).start()
        xy_buf[i, xy] = half[i, 0]

    def sum_z(i):
        drain(xy_buf.at[i, 0:15], ar_recv.at[4 * i + 1])
        half[i, 1] = tree_sum([xy_buf[i, k] for k in range(16)])
        for k in range(1, HEIGHT):
            remote(
                half.at[i, 1], z_buf.at[i, z], ar_send.at[4 * i + 2], ar_recv.at[4 * i + 2],
                (r, (z + k) % HEIGHT),
            ).start()
        z_buf[i, z] = half[i, 1]

    def sum_c(i):
        drain(z_buf.at[i, 0:7], ar_recv.at[4 * i + 2])
        here = whole.at[i, pl.ds(pl.multiple_of(c * 16, 16), 16)]
        here[...] = tree_sum([z_buf[i, k] for k in range(HEIGHT)])
        remote(here, here, ar_send.at[4 * i + 3], ar_recv.at[4 * i + 3], partner).start()

    def sum_end(i):
        there = whole.at[i, pl.ds(pl.multiple_of((1 - c) * 16, 16), 16)]
        drain(there, ar_recv.at[4 * i + 3])
        return unpack(whole[i])

    a = acc[...]
    cross = a[0:64, 64:128] + a[0:64, 128:192]
    gram = (a[0:64, 0:64] + (cross + cross.T) + a[64:128, 64:128]) * (1.0 / CELLS)
    sum_start(0, pack(gram))

    for i in range(4):
        drain(faces.at[4 + i] if i < 2 else faces.at[4 + i, 0:8], fx_recv.at[i])
    row_id = lax.broadcasted_iota(jnp.int32, (NZL, NY), 0)
    lane_id = lax.broadcasted_iota(jnp.int32, (NZL, NY), 1)
    ok_lo_x = jnp.where(r > 0, 1.0, 0.0).astype(F32)
    ok_hi_x = jnp.where(r < ROWS - 1, 1.0, 0.0).astype(F32)
    ok_lo_z = jnp.where(z > 0, 1.0, 0.0).astype(F32)
    ok_hi_z = jnp.where(z < HEIGHT - 1, 1.0, 0.0).astype(F32)
    for x in range(NXL):
        cc = cond[x]
        couple = lookup(mat[x], COUPLE_TABLE)
        half_c = 0.5 * cc
        diag = couple
        if x == 0:
            lo = 0.5 * (cc + faces[4]) * ok_lo_x
            diag = diag + half_c * (1.0 - ok_lo_x)
        else:
            lo = 0.5 * (cc + cond[x - 1])
        if x == NXL - 1:
            hi = 0.5 * (cc + faces[5]) * ok_hi_x
            diag = diag + half_c * (1.0 - ok_hi_x)
        else:
            hi = 0.5 * (cc + cond[x + 1])
        below = jnp.concatenate([faces[6, x : x + 1], cc[0 : NZL - 1]], axis=0)
        above = jnp.concatenate([cc[1:NZL], faces[7, x : x + 1]], axis=0)
        mask_lo = jnp.where(row_id == 0, ok_lo_z, 1.0)
        mask_hi = jnp.where(row_id == NZL - 1, ok_hi_z, 1.0)
        zlo = 0.5 * (cc + below) * mask_lo
        zhi = 0.5 * (cc + above) * mask_hi
        diag = diag + half_c * ((1.0 - mask_lo) + (1.0 - mask_hi))
        nxt = pltpu.roll(cc, NY - 1, 1)
        ly = jnp.where(lane_id == NY - 1, 0.0, 0.5 * (cc + nxt))
        edge = jnp.where((lane_id == 0) | (lane_id == NY - 1), half_c, 0.0)
        coef[0, x] = diag + edge
        coef[1, x] = lo
        coef[2, x] = hi
        coef[3, x] = zlo
        coef[4, x] = zhi
        coef[5, x] = ly

    sum_xy(0)

    def image(x, z0, z1, part):
        def at(xx, zz):
            return lay[xx, part, zsl(zz)]

        v = at(x + 1, z0)
        prev = hz_lo[x, part] if z0 == 0 else at(x + 1, z0 - 1)
        flux = coef[3, x, z0 : z0 + 1, :] * (prev - v)
        for zz in range(z0, z1):
            nxt = hz_hi[x, part] if zz == NZL - 1 else at(x + 1, zz + 1)

            def cf(i):
                return coef[i, x, zz : zz + 1, :]

            q = cf(5) * (v - pltpu.roll(v, NY - 1, 1))
            out = cf(0) * v - flux
            out += cf(1) * (v - at(x, zz))
            out += cf(2) * (v - at(x + 2, zz))
            flux = cf(4) * (v - nxt)
            out += flux + (q - pltpu.roll(q, 1, 1))
            for k, piece in enumerate(split3(out)):
                i3[x, k * M + part.start : k * M + part.stop, zsl(zz)] = piece
            v = nxt

    def images(x, z0, z1):
        for part in PARTS:
            image(x, z0, z1, part)

    def inner_body(x, carry):
        images(x, 1, NZL - 1)
        cells = slice(NY, LANES - NY)
        acc2[...] += nt_dot(f3[x, :, cells], i3[x, :, cells])
        return carry

    lax.fori_loop(1, NXL - 1, inner_body, 0)

    def outer():
        drain(hz_lo, fx_recv.at[4])
        drain(hz_hi, fx_recv.at[5])
        drain(lay.at[NXL + 1], fx_recv.at[6])
        drain(lay.at[0], fx_recv.at[7])

        def end_body(i, carry):
            x = i * (NXL - 1)
            images(x, 0, NZL)
            acc2[...] += nt_dot(f3[x], i3[x])
            return carry

        def edge_body(x, carry):
            images(x, 0, 1)
            images(x, NZL - 1, NZL)

            def both(ref):
                return jnp.concatenate([ref[x, :, zsl(0)], ref[x, :, zsl(NZL - 1)]], axis=1)

            acc2[...] += nt_dot(both(f3), both(i3))
            return carry

        lax.fori_loop(0, 2, end_body, 0)
        sum_z(0)
        lax.fori_loop(1, NXL - 1, edge_body, 0)

    outer()

    a = acc2[...]
    proj = (
        a[0:64, 0:64]
        + (a[0:64, 64:128] + a[64:128, 0:64])
        + (a[0:64, 128:192] + a[64:128, 64:128] + a[128:192, 0:64])
    ) * (1.0 / CELLS)
    sum_start(1, pack(proj))
    sum_xy(1)
    sum_c(0)
    g = sum_end(0)

    ri = lax.broadcasted_iota(jnp.int32, (M, M), 0)
    ci = lax.broadcasted_iota(jnp.int32, (M, M), 1)
    w = eliminate(jnp.concatenate([g, jnp.where(ri == ci, 1.0, 0.0).astype(F32)], axis=1))
    u = w[:, 0:M]
    d = jnp.sum(jnp.where(ri == ci, u, 0.0), axis=1, keepdims=True)
    rs = lax.rsqrt(d)
    linv = jnp.where(ci <= ri, w[:, M : 2 * M] * rs, 0.0)
    upper = jnp.where(ci >= ri, u * rs, 0.0)
    w_out[...] = jnp.concatenate([upper, linv], axis=1)
    h, m, low = split3(linv)
    zero = jnp.zeros_like(h)
    lst[0:64] = jnp.concatenate([h, h, h, m], axis=1)
    lst[64:128] = jnp.concatenate([low, m, zero, zero], axis=1)
    sum_z(1)

    step = 512

    def inverse_body(x, carry):
        for src, dst in ((f3, basis_v), (i3, applied_v)):
            out = dst.at[x].reshape(M * NZL, NY)
            for col in range(0, LANES, step):
                cells = slice(col, col + step)
                rhs = jnp.concatenate([src[x, :, cells], src[x, 0:64, cells]], axis=0)
                p = jnp.dot(lst[...], rhs, preferred_element_type=F32)
                p = p[0:64] + p[64:128]
                for k in range(step // NY):
                    out[pl.ds(col // NY + k, M, stride=NZL), :] = p[:, k * NY : (k + 1) * NY]
        return carry

    lax.fori_loop(0, NXL, inverse_body, 0)
    sum_c(1)

    for i in range(4):
        drain(faces.at[4] if i < 2 else faces.at[4, 0:8], fx_send.at[i])
    drain(hz_lo, fx_send.at[4])
    drain(hz_hi, fx_send.at[5])
    drain(lay.at[0], fx_send.at[6])
    drain(lay.at[0], fx_send.at[7])
    for i in range(2):
        drain(from_c.at[i], ar_send.at[4 * i])
        drain(xy_buf.at[i, 0:15], ar_send.at[4 * i + 1])
        drain(z_buf.at[i, 0:7], ar_send.at[4 * i + 2])
        drain(from_c.at[i], ar_send.at[4 * i + 3])
    pt_out[...] = sum_end(1)


def last_kernel(basis_v, applied_v, w_in, pt, basis, applied, reduced, low_factor, sem):
    for x in range(NXL):
        pltpu.make_async_copy(basis_v.at[x], basis.at[:, x], sem).start()
    for x in range(NXL):
        pltpu.make_async_copy(applied_v.at[x], applied.at[:, x], sem).start()
    w = w_in[...]
    linv = w[:, M : 2 * M]
    low_factor[...] = w[:, 0:M].T
    hi = lax.Precision.HIGHEST
    t = jnp.dot(linv, pt[...], precision=hi, preferred_element_type=F32)
    reduced[...] = lax.dot_general(
        t, linv, (((1,), (1,)), ((), ())), precision=hi, preferred_element_type=F32
    )
    pltpu.make_async_copy(basis_v, basis_v, sem).wait()
    pltpu.make_async_copy(applied_v, applied_v, sem).wait()


def local(snapshots, material):
    any_ = pl.BlockSpec(memory_space=pl.ANY)
    vm = pl.BlockSpec(memory_space=pltpu.VMEM)
    dma, fbuf = pltpu.SemaphoreType.DMA, functools.partial(pltpu.VMEM, dtype=F32)
    wide = pltpu.VMEM((NXL, 192, LANES), BF16)
    held = fbuf((NXL, M, NZL, NY))
    basis_v, applied_v, w, pt = pl.pallas_call(
        first_kernel,
        out_shape=(held, held, fbuf((M, 2 * M)), fbuf((M, M))),
        in_specs=[any_, any_],
        out_specs=(vm, vm, vm, vm),
        scratch_shapes=[
            pltpu.VMEM((NXL, NZL, NY), jnp.int32),
            fbuf((NXL, M, NZL, NY)),
            fbuf((NXL + 2, M, LANES)),
            wide,
            wide,
            fbuf((2, NXL, M, NY)),
            fbuf((NXL, M, NY)),
            fbuf((NXL, M, NY)),
            fbuf((NXL, NZL, NY)),
            fbuf((8, NZL, NY)),
            fbuf((6, NXL, NZL, NY)),
            fbuf((128, 192)),
            fbuf((192, 192)),
            fbuf((2, 32, 128)),
            fbuf((2, 16, 128)),
            fbuf((2, 16, 16, 128)),
            fbuf((2, 8, 16, 128)),
            fbuf((2, 2, 16, 128)),
            fbuf((2, 32, 128)),
            pltpu.VMEM((128, 256), BF16),
            dma((NXL + 1,)),
            dma((8,)),
            dma((8,)),
            dma((8,)),
            dma((8,)),
        ],
        compiler_params=pltpu.CompilerParams(
            collective_id=0, has_side_effects=True, vmem_limit_bytes=32 << 20
        ),
        name="gram_and_image",
    )(
        pltpu.with_memory_space_constraint(snapshots, pltpu.HBM),
        pltpu.with_memory_space_constraint(material, pltpu.HBM),
    )
    full = jax.ShapeDtypeStruct((M, NXL, NZL, NY), F32)
    small = jax.ShapeDtypeStruct((M, M), F32)
    return pl.pallas_call(
        last_kernel,
        out_shape=(full, full, small, small),
        in_specs=[vm, vm, vm, vm],
        out_specs=(any_, any_, vm, vm),
        scratch_shapes=[dma],
        compiler_params=pltpu.CompilerParams(vmem_limit_bytes=8 << 20),
        name="write_results",
    )(basis_v, applied_v, w, pt)


def solution(mesh):
    in_specs = (P(None, "rows", "height", None), P("rows", "height", None))
    out_specs = (P(None, "rows", "height", None), P(None, "rows", "height", None), P(), P())
    return jax.shard_map(local, mesh=mesh, in_specs=in_specs, out_specs=out_specs, check_vma=False)
```

```python
import functools

import jax
import jax.numpy as jnp
from jax import lax
from jax.experimental import pallas as pl
from jax.experimental.pallas import tpu as pltpu
from jax.sharding import PartitionSpec as P

CONDUCT_TABLE = (0.5, 2.0, 1.0)
COUPLE_TABLE = (0.3, 0.1, 0.6)
MESH = pl.DeviceIdType.MESH
F32 = jnp.float32
BF16 = jnp.bfloat16
M = 64
NXL, NZL, NY = 8, 16, 128
LANES = NZL * NY
ROWS, HEIGHT = 32, 8
CELLS = 4194304
PARTS = (slice(0, 64),)


def lookup(material, table):
    return jnp.where(material == 0, table[0], jnp.where(material == 1, table[1], table[2])).astype(F32)


def split3(f):
    h = f.astype(BF16)
    r = f - h.astype(F32)
    m = r.astype(BF16)
    return h, m, (r - m.astype(F32)).astype(BF16)


def tree_sum(vals):
    while len(vals) > 1:
        vals = [vals[i] + vals[i + 1] if i + 1 < len(vals) else vals[i] for i in range(0, len(vals), 2)]
    return vals[0]


def zsl(z):
    return slice(z * NY, (z + 1) * NY)


def square_ids(rows, cols):
    return (
        lax.broadcasted_iota(jnp.int32, (rows, cols), 0),
        lax.broadcasted_iota(jnp.int32, (rows, cols), 1),
    )


def pack(g):
    ri, ci = square_ids(32, M)
    lower = jnp.concatenate([g[32:64, 32:64], g[32:64, 0:32]], axis=1)
    both = jnp.where(ri > ci, lower, g[0:32])
    diag = jnp.sum(jnp.where(ri + 32 == ci, g[32:64], 0.0), axis=0, keepdims=True)
    diag = jnp.concatenate([diag, diag], axis=1)
    return [
        jnp.concatenate([both[k : k + 8], both[k + 8 : k + 16]], axis=1) for k in (0, 16)
    ], diag


def unpack(halves, diag):
    both = jnp.concatenate([p for h in halves for p in (h[:, 0:M], h[:, M : 2 * M])], axis=0)
    ri, ci = square_ids(32, M)
    upper = jnp.where(ri < ci, both, 0.0)
    lower = jnp.where(ri > ci, both, 0.0)
    lower = jnp.concatenate([lower[:, 32:64], lower[:, 0:32]], axis=1)
    off = jnp.concatenate([upper, lower], axis=0)
    on = jnp.concatenate(
        [jnp.where(ri == ci, both, 0.0), jnp.where(ri + 32 == ci, diag[:, 0:M], 0.0)], axis=0
    )
    return off + off.T + on


def nt_dot(a, b):
    return lax.dot_general(a, b, (((1,), (1,)), ((), ())), preferred_element_type=F32)


def eliminate(w):
    blocks = [w[8 * k : 8 * k + 8] for k in range(8)]
    rid = lax.broadcasted_iota(jnp.int32, (8, 2 * M), 0)

    def over_lanes(v, j):
        return jnp.broadcast_to(v[:, j : j + 1], (8, 2 * M))

    def over_rows(v, s):
        return jnp.broadcast_to(v[s : s + 1, :], (8, 2 * M))

    for b in range(8):
        full = upper = blocks[b]
        cols = [over_lanes(full, 8 * b + s) for s in range(8)]
        below = [[over_lanes(blocks[k], 8 * b + s) for s in range(8)] for k in range(b + 1, 8)]
        for s in range(8):
            inv = 1.0 / over_rows(cols[s], s)
            here = rid == s
            mult = cols[s] * inv
            upper = jnp.where(here, full, upper)
            full = jnp.where(here, full * inv, full - mult * over_rows(full, s))
            for t in range(s + 1, 8):
                cols[t] = jnp.where(here, cols[t] * inv, cols[t] - mult * over_rows(cols[t], s))
        rows = [over_rows(full, s) for s in range(8)]
        for k in range(b + 1, 8):
            blocks[k] = blocks[k] - tree_sum([below[k - b - 1][s] * rows[s] for s in range(8)])
        blocks[b] = upper
    return jnp.concatenate(blocks, axis=0)


def first_kernel(
    snap, mat_in, basis_v, applied_v, w_out, pt_out,
    mat, fld, lay, f3, i3, hz_lo, hz_hi, cond, faces, coef, acc, acc2,
    mine, rows_buf, z_buf, half, lst,
    load_sem, fx_send, fx_recv, ar_send, ar_recv,
):
    r = lax.axis_index("rows")
    z = lax.axis_index("height")
    xy, c = r // 2, r % 2
    up_r, dn_r = (r + 1) % ROWS, (r + ROWS - 1) % ROWS
    up_z, dn_z = (z + 1) % HEIGHT, (z + HEIGHT - 1) % HEIGHT

    def remote(src, dst, ss, rs, dev):
        return pltpu.make_async_remote_copy(
            src_ref=src, dst_ref=dst, send_sem=ss, recv_sem=rs, device_id=dev, device_id_type=MESH
        )

    def drain(ref, sem):
        pltpu.make_async_copy(ref, ref, sem).wait()

    def slab(x, zz):
        return fld.at[x].reshape(M * NZL, NY)[pl.ds(zz, M, stride=NZL), :]

    pltpu.make_async_copy(mat_in, mat, load_sem.at[NXL]).start()
    for x in (0, NXL - 1, *range(1, NXL - 1)):
        pltpu.make_async_copy(snap.at[:, x], fld.at[x], load_sem.at[x]).start()

    bar = pltpu.get_barrier_semaphore()

    def greet(dev):
        pl.semaphore_signal(bar, inc=1, device_id=dev, device_id_type=MESH)

    for k in range(1, ROWS):
        greet(((r + k) % ROWS, z))
    for k in range(1, HEIGHT):
        greet((r, (z + k) % HEIGHT))
        greet((xy * 2 + (1 - c), (z + k) % HEIGHT))

    drain(mat, load_sem.at[NXL])
    cond[...] = lookup(mat[...], CONDUCT_TABLE)
    faces[0] = cond[NXL - 1]
    faces[1] = cond[0]
    faces[2, 0:8] = cond[:, NZL - 1, :]
    faces[3, 0:8] = cond[:, 0, :]
    pl.semaphore_wait(bar, ROWS - 1 + 2 * (HEIGHT - 1))
    remote(faces.at[0], faces.at[4], fx_send.at[0], fx_recv.at[0], (up_r, z)).start()
    remote(faces.at[1], faces.at[5], fx_send.at[1], fx_recv.at[1], (dn_r, z)).start()
    remote(faces.at[2, 0:8], faces.at[6, 0:8], fx_send.at[2], fx_recv.at[2], (r, up_z)).start()
    remote(faces.at[3, 0:8], faces.at[7, 0:8], fx_send.at[3], fx_recv.at[3], (r, dn_z)).start()

    def face_body(x, carry):
        remote(
            snap.at[:, x, NZL - 1, :], hz_lo.at[x], fx_send.at[4], fx_recv.at[4], (r, up_z)
        ).start()
        remote(snap.at[:, x, 0, :], hz_hi.at[x], fx_send.at[5], fx_recv.at[5], (r, dn_z)).start()
        return carry

    for zz in range(NZL):
        remote(
            snap.at[:, 0, zz, :], lay.at[NXL + 1, :, zsl(zz)], fx_send.at[6], fx_recv.at[6],
            (dn_r, z),
        ).start()
        remote(
            snap.at[:, NXL - 1, zz, :], lay.at[0, :, zsl(zz)], fx_send.at[7], fx_recv.at[7],
            (up_r, z),
        ).start()
    lax.fori_loop(0, NXL, face_body, 0)
    acc[...] = jnp.zeros_like(acc)
    acc2[...] = jnp.zeros_like(acc2)

    def gram_part(x):
        for zz in range(NZL):
            v = slab(x, zz)
            lay[x + 1, :, zsl(zz)] = v
            h, m, low = split3(v)
            f3[x, 0:64, zsl(zz)] = h
            f3[x, 64:128, zsl(zz)] = m
            f3[x, 128:192, zsl(zz)] = low
        acc[...] += nt_dot(f3[x, 0:128], f3[x])

    drain(fld.at[0], load_sem.at[0])
    gram_part(0)
    drain(fld.at[NXL - 1], load_sem.at[NXL - 1])

    gram_part(NXL - 1)

    def gram_body(x, carry):
        drain(fld.at[x], load_sem.at[x])
        gram_part(x)
        return carry

    lax.fori_loop(1, NXL - 1, gram_body, 0)

    def sum_rows(i, value):
        halves, diag = value
        for h in range(2):
            mine[i, h, 0:8] = halves[h]
            mine[i, h, 8:9] = diag
        for k in range(1, ROWS):
            to = (r + k) % ROWS
            remote(
                mine.at[i, to % 2], rows_buf.at[i, r], ar_send.at[2 * i], ar_recv.at[2 * i], (to, z)
            ).start()
        rows_buf[i, r] = mine[i, c]

    def sum_z(i):
        drain(rows_buf.at[i, 0 : ROWS - 1], ar_recv.at[2 * i])
        half[i] = tree_sum([rows_buf[i, k] for k in range(ROWS)])
        slot = c * HEIGHT + z
        for k in range(1, 2 * HEIGHT):
            to = (slot + k) % (2 * HEIGHT)
            remote(
                half.at[i], z_buf.at[i, slot], ar_send.at[2 * i + 1], ar_recv.at[2 * i + 1],
                (xy * 2 + to // HEIGHT, to % HEIGHT),
            ).start()
        z_buf[i, slot] = half[i]

    def sum_end(i):
        drain(z_buf.at[i, 0 : 2 * HEIGHT - 1], ar_recv.at[2 * i + 1])
        halves = [
            tree_sum([z_buf[i, h * HEIGHT + k, 0:8] for k in range(HEIGHT)]) for h in range(2)
        ]
        diag = tree_sum([z_buf[i, k, 8:9] for k in range(HEIGHT)])
        return unpack(halves, diag)

    a = acc[...]
    cross = a[0:64, 64:128] + a[0:64, 128:192]
    gram = (a[0:64, 0:64] + (cross + cross.T) + a[64:128, 64:128]) * (1.0 / CELLS)
    sum_rows(0, pack(gram))

    for i in range(4):
        drain(faces.at[4 + i] if i < 2 else faces.at[4 + i, 0:8], fx_recv.at[i])
    row_id = lax.broadcasted_iota(jnp.int32, (NZL, NY), 0)
    lane_id = lax.broadcasted_iota(jnp.int32, (NZL, NY), 1)
    ok_lo_x = jnp.where(r > 0, 1.0, 0.0).astype(F32)
    ok_hi_x = jnp.where(r < ROWS - 1, 1.0, 0.0).astype(F32)
    ok_lo_z = jnp.where(z > 0, 1.0, 0.0).astype(F32)
    ok_hi_z = jnp.where(z < HEIGHT - 1, 1.0, 0.0).astype(F32)
    for x in range(NXL):
        cc = cond[x]
        couple = lookup(mat[x], COUPLE_TABLE)
        half_c = 0.5 * cc
        diag = couple
        if x == 0:
            lo = 0.5 * (cc + faces[4]) * ok_lo_x
            diag = diag + half_c * (1.0 - ok_lo_x)
        else:
            lo = 0.5 * (cc + cond[x - 1])
        if x == NXL - 1:
            hi = 0.5 * (cc + faces[5]) * ok_hi_x
            diag = diag + half_c * (1.0 - ok_hi_x)
        else:
            hi = 0.5 * (cc + cond[x + 1])
        below = jnp.concatenate([faces[6, x : x + 1], cc[0 : NZL - 1]], axis=0)
        above = jnp.concatenate([cc[1:NZL], faces[7, x : x + 1]], axis=0)
        mask_lo = jnp.where(row_id == 0, ok_lo_z, 1.0)
        mask_hi = jnp.where(row_id == NZL - 1, ok_hi_z, 1.0)
        zlo = 0.5 * (cc + below) * mask_lo
        zhi = 0.5 * (cc + above) * mask_hi
        diag = diag + half_c * ((1.0 - mask_lo) + (1.0 - mask_hi))
        nxt = pltpu.roll(cc, NY - 1, 1)
        ly = jnp.where(lane_id == NY - 1, 0.0, 0.5 * (cc + nxt))
        edge = jnp.where((lane_id == 0) | (lane_id == NY - 1), half_c, 0.0)
        coef[0, x] = diag + edge
        coef[1, x] = lo
        coef[2, x] = hi
        coef[3, x] = zlo
        coef[4, x] = zhi
        coef[5, x] = ly


    def image(x, z0, z1, part):
        def at(xx, zz):
            return lay[xx, part, zsl(zz)]

        v = at(x + 1, z0)
        prev = hz_lo[x, part] if z0 == 0 else at(x + 1, z0 - 1)
        flux = coef[3, x, z0 : z0 + 1, :] * (prev - v)
        for zz in range(z0, z1):
            nxt = hz_hi[x, part] if zz == NZL - 1 else at(x + 1, zz + 1)

            def cf(i):
                return coef[i, x, zz : zz + 1, :]

            q = cf(5) * (v - pltpu.roll(v, NY - 1, 1))
            out = cf(0) * v - flux
            out += cf(1) * (v - at(x, zz))
            out += cf(2) * (v - at(x + 2, zz))
            flux = cf(4) * (v - nxt)
            out += flux + (q - pltpu.roll(q, 1, 1))
            for k, piece in enumerate(split3(out)):
                i3[x, k * M + part.start : k * M + part.stop, zsl(zz)] = piece
            v = nxt

    def images(x, z0, z1):
        for part in PARTS:
            image(x, z0, z1, part)

    def inner_body(x, carry):
        images(x, 1, NZL - 1)
        cells = slice(NY, LANES - NY)
        acc2[...] += nt_dot(f3[x, :, cells], i3[x, :, cells])
        return carry

    lax.fori_loop(1, NXL - 1, inner_body, 0)

    def outer():
        drain(hz_lo, fx_recv.at[4])
        drain(hz_hi, fx_recv.at[5])
        drain(lay.at[NXL + 1], fx_recv.at[6])
        drain(lay.at[0], fx_recv.at[7])

        def end_body(i, carry):
            x = i * (NXL - 1)
            images(x, 0, NZL)
            acc2[...] += nt_dot(f3[x], i3[x])
            return carry

        def edge_image(x, carry):
            images(x, 0, 1)
            images(x, NZL - 1, NZL)
            return carry

        def edges(ref):
            return jnp.concatenate(
                [ref[x, :, zsl(zz)] for x in range(1, NXL - 1) for zz in (0, NZL - 1)], axis=1
            )

        lax.fori_loop(1, NXL - 1, edge_image, 0)
        acc2[...] += nt_dot(edges(f3), edges(i3))
        sum_z(0)
        lax.fori_loop(0, 2, end_body, 0)

    outer()

    a = acc2[...]
    proj = (
        a[0:64, 0:64]
        + (a[0:64, 64:128] + a[64:128, 0:64])
        + (a[0:64, 128:192] + a[64:128, 64:128] + a[128:192, 0:64])
    ) * (1.0 / CELLS)
    sum_rows(1, pack(0.5 * (proj + proj.T)))
    g = sum_end(0)

    ri = lax.broadcasted_iota(jnp.int32, (M, M), 0)
    ci = lax.broadcasted_iota(jnp.int32, (M, M), 1)
    w = eliminate(jnp.concatenate([g, jnp.where(ri == ci, 1.0, 0.0).astype(F32)], axis=1))
    u = w[:, 0:M]
    d = jnp.sum(jnp.where(ri == ci, u, 0.0), axis=1, keepdims=True)
    rs = lax.rsqrt(d)
    linv = jnp.where(ci <= ri, w[:, M : 2 * M] * rs, 0.0)
    upper = jnp.where(ci >= ri, u * rs, 0.0)
    w_out[...] = jnp.concatenate([upper, linv], axis=1)
    h, m, low = split3(linv)
    zero = jnp.zeros_like(h)
    lst[0:64] = jnp.concatenate([h, h, h, m], axis=1)
    lst[64:128] = jnp.concatenate([low, m, zero, zero], axis=1)
    sum_z(1)

    step = 512

    def inverse_body(x, carry):
        for src, dst in ((f3, basis_v), (i3, applied_v)):
            out = dst.at[x].reshape(M * NZL, NY)
            for col in range(0, LANES, step):
                cells = slice(col, col + step)
                rhs = jnp.concatenate([src[x, :, cells], src[x, 0:64, cells]], axis=0)
                p = jnp.dot(lst[...], rhs, preferred_element_type=F32)
                p = p[0:64] + p[64:128]
                for k in range(step // NY):
                    out[pl.ds(col // NY + k, M, stride=NZL), :] = p[:, k * NY : (k + 1) * NY]
        return carry

    lax.fori_loop(0, NXL, inverse_body, 0)

    for i in range(4):
        drain(faces.at[4] if i < 2 else faces.at[4, 0:8], fx_send.at[i])
    drain(hz_lo, fx_send.at[4])
    drain(hz_hi, fx_send.at[5])
    drain(lay.at[0], fx_send.at[6])
    drain(lay.at[0], fx_send.at[7])
    for i in range(2):
        drain(rows_buf.at[i, 0 : ROWS - 1], ar_send.at[2 * i])
        drain(z_buf.at[i, 0 : 2 * HEIGHT - 1], ar_send.at[2 * i + 1])
    pt_out[...] = sum_end(1)


def last_kernel(basis_v, applied_v, w_in, pt, basis, applied, reduced, low_factor, sem):
    for x in range(NXL):
        pltpu.make_async_copy(basis_v.at[x], basis.at[:, x], sem).start()
    for x in range(NXL):
        pltpu.make_async_copy(applied_v.at[x], applied.at[:, x], sem).start()
    w = w_in[...]
    linv = w[:, M : 2 * M]
    low_factor[...] = w[:, 0:M].T
    hi = lax.Precision.HIGHEST
    t = jnp.dot(linv, pt[...], precision=hi, preferred_element_type=F32)
    reduced[...] = lax.dot_general(
        t, linv, (((1,), (1,)), ((), ())), precision=hi, preferred_element_type=F32
    )
    pltpu.make_async_copy(basis_v, basis_v, sem).wait()
    pltpu.make_async_copy(applied_v, applied_v, sem).wait()


def local(snapshots, material):
    any_ = pl.BlockSpec(memory_space=pl.ANY)
    vm = pl.BlockSpec(memory_space=pltpu.VMEM)
    dma, fbuf = pltpu.SemaphoreType.DMA, functools.partial(pltpu.VMEM, dtype=F32)
    wide = pltpu.VMEM((NXL, 192, LANES), BF16)
    held = fbuf((NXL, M, NZL, NY))
    basis_v, applied_v, w, pt = pl.pallas_call(
        first_kernel,
        out_shape=(held, held, fbuf((M, 2 * M)), fbuf((M, M))),
        in_specs=[any_, any_],
        out_specs=(vm, vm, vm, vm),
        scratch_shapes=[
            pltpu.VMEM((NXL, NZL, NY), jnp.int32),
            fbuf((NXL, M, NZL, NY)),
            fbuf((NXL + 2, M, LANES)),
            wide,
            wide,
            fbuf((NXL, M, NY)),
            fbuf((NXL, M, NY)),
            fbuf((NXL, NZL, NY)),
            fbuf((8, NZL, NY)),
            fbuf((6, NXL, NZL, NY)),
            fbuf((128, 192)),
            fbuf((192, 192)),
            fbuf((2, 2, 9, 128)),
            fbuf((2, ROWS, 9, 128)),
            fbuf((2, 2 * HEIGHT, 9, 128)),
            fbuf((2, 9, 128)),
            pltpu.VMEM((128, 256), BF16),
            dma((NXL + 1,)),
            dma((8,)),
            dma((8,)),
            dma((4,)),
            dma((4,)),
        ],
        compiler_params=pltpu.CompilerParams(
            collective_id=0, has_side_effects=True, vmem_limit_bytes=32 << 20
        ),
        name="gram_and_image",
    )(
        pltpu.with_memory_space_constraint(snapshots, pltpu.HBM),
        pltpu.with_memory_space_constraint(material, pltpu.HBM),
    )
    full = jax.ShapeDtypeStruct((M, NXL, NZL, NY), F32)
    small = jax.ShapeDtypeStruct((M, M), F32)
    return pl.pallas_call(
        last_kernel,
        out_shape=(full, full, small, small),
        in_specs=[vm, vm, vm, vm],
        out_specs=(any_, any_, vm, vm),
        scratch_shapes=[dma],
        compiler_params=pltpu.CompilerParams(vmem_limit_bytes=8 << 20),
        name="write_results",
    )(basis_v, applied_v, w, pt)


def solution(mesh):
    in_specs = (P(None, "rows", "height", None), P("rows", "height", None))
    out_specs = (P(None, "rows", "height", None), P(None, "rows", "height", None), P(), P())
    return jax.shard_map(local, mesh=mesh, in_specs=in_specs, out_specs=out_specs, check_vma=False)
```

```python
import functools

import jax
import jax.numpy as jnp
from jax import lax
from jax.experimental import pallas as pl
from jax.experimental.pallas import tpu as pltpu
from jax.sharding import PartitionSpec as P

CONDUCT_TABLE = (0.5, 2.0, 1.0)
COUPLE_TABLE = (0.3, 0.1, 0.6)
MESH = pl.DeviceIdType.MESH
F32 = jnp.float32
BF16 = jnp.bfloat16
M = 64
NXL, NZL, NY = 8, 16, 128
LANES = NZL * NY
ROWS, HEIGHT = 32, 8
CELLS = 4194304
PARTS = (slice(0, 64),)


def lookup(material, table):
    return jnp.where(material == 0, table[0], jnp.where(material == 1, table[1], table[2])).astype(F32)


def split3(f):
    h = f.astype(BF16)
    r = f - h.astype(F32)
    m = r.astype(BF16)
    return h, m, (r - m.astype(F32)).astype(BF16)


def tree_sum(vals):
    while len(vals) > 1:
        vals = [vals[i] + vals[i + 1] if i + 1 < len(vals) else vals[i] for i in range(0, len(vals), 2)]
    return vals[0]


def zsl(z):
    return slice(z * NY, (z + 1) * NY)


def square_ids(rows, cols):
    return (
        lax.broadcasted_iota(jnp.int32, (rows, cols), 0),
        lax.broadcasted_iota(jnp.int32, (rows, cols), 1),
    )


def pack(g):
    ri, ci = square_ids(32, M)
    lower = jnp.concatenate([g[32:64, 32:64], g[32:64, 0:32]], axis=1)
    both = jnp.where(ri > ci, lower, g[0:32])
    diag = jnp.sum(jnp.where(ri + 32 == ci, g[32:64], 0.0), axis=0, keepdims=True)
    diag = jnp.concatenate([diag, diag], axis=1)
    return [
        jnp.concatenate([both[k : k + 8], both[k + 8 : k + 16]], axis=1) for k in (0, 16)
    ], diag


def unpack(halves, diag):
    both = jnp.concatenate([p for h in halves for p in (h[:, 0:M], h[:, M : 2 * M])], axis=0)
    ri, ci = square_ids(32, M)
    upper = jnp.where(ri < ci, both, 0.0)
    lower = jnp.where(ri > ci, both, 0.0)
    lower = jnp.concatenate([lower[:, 32:64], lower[:, 0:32]], axis=1)
    off = jnp.concatenate([upper, lower], axis=0)
    on = jnp.concatenate(
        [jnp.where(ri == ci, both, 0.0), jnp.where(ri + 32 == ci, diag[:, 0:M], 0.0)], axis=0
    )
    return off + off.T + on


def nt_dot(a, b):
    return lax.dot_general(a, b, (((1,), (1,)), ((), ())), preferred_element_type=F32)


def eliminate(w):
    blocks = [w[8 * k : 8 * k + 8] for k in range(8)]
    rid = lax.broadcasted_iota(jnp.int32, (8, 2 * M), 0)

    def over_lanes(v, j):
        return jnp.broadcast_to(v[:, j : j + 1], (8, 2 * M))

    def over_rows(v, s):
        return jnp.broadcast_to(v[s : s + 1, :], (8, 2 * M))

    for b in range(8):
        full = upper = blocks[b]
        cols = [over_lanes(full, 8 * b + s) for s in range(8)]
        below = [[over_lanes(blocks[k], 8 * b + s) for s in range(8)] for k in range(b + 1, 8)]
        for s in range(8):
            inv = 1.0 / over_rows(cols[s], s)
            here = rid == s
            mult = cols[s] * inv
            upper = jnp.where(here, full, upper)
            full = jnp.where(here, full * inv, full - mult * over_rows(full, s))
            for t in range(s + 1, 8):
                cols[t] = jnp.where(here, cols[t] * inv, cols[t] - mult * over_rows(cols[t], s))
        rows = [over_rows(full, s) for s in range(8)]
        for k in range(b + 1, 8):
            blocks[k] = blocks[k] - tree_sum([below[k - b - 1][s] * rows[s] for s in range(8)])
        blocks[b] = upper
    return jnp.concatenate(blocks, axis=0)


def first_kernel(
    snap, mat_in, basis_v, applied_v, w_out, pt_out,
    mat, fld, lay, f3, i3, hz_lo, hz_hi, cond, faces, coef, acc, acc2,
    mine, rows_buf, z_buf, half, lst,
    load_sem, fx_send, fx_recv, ar_send, ar_recv,
):
    r = lax.axis_index("rows")
    z = lax.axis_index("height")
    xy, c = r // 2, r % 2
    up_r, dn_r = (r + 1) % ROWS, (r + ROWS - 1) % ROWS
    up_z, dn_z = (z + 1) % HEIGHT, (z + HEIGHT - 1) % HEIGHT

    def remote(src, dst, ss, rs, dev):
        return pltpu.make_async_remote_copy(
            src_ref=src, dst_ref=dst, send_sem=ss, recv_sem=rs, device_id=dev, device_id_type=MESH
        )

    def drain(ref, sem):
        pltpu.make_async_copy(ref, ref, sem).wait()

    def slab(x, zz):
        return fld.at[x].reshape(M * NZL, NY)[pl.ds(zz, M, stride=NZL), :]

    pltpu.make_async_copy(mat_in, mat, load_sem.at[NXL]).start()
    for x in (0, NXL - 1, *range(1, NXL - 1)):
        pltpu.make_async_copy(snap.at[:, x], fld.at[x], load_sem.at[x]).start()

    bar = pltpu.get_barrier_semaphore()

    def greet(dev):
        pl.semaphore_signal(bar, inc=1, device_id=dev, device_id_type=MESH)

    for k in range(1, ROWS):
        greet(((r + k) % ROWS, z))
    for k in range(1, HEIGHT):
        greet((r, (z + k) % HEIGHT))
        greet((xy * 2 + (1 - c), (z + k) % HEIGHT))

    drain(mat, load_sem.at[NXL])
    cond[...] = lookup(mat[...], CONDUCT_TABLE)
    faces[0] = cond[NXL - 1]
    faces[1] = cond[0]
    faces[2, 0:8] = cond[:, NZL - 1, :]
    faces[3, 0:8] = cond[:, 0, :]
    pl.semaphore_wait(bar, ROWS - 1 + 2 * (HEIGHT - 1))
    remote(faces.at[0], faces.at[4], fx_send.at[0], fx_recv.at[0], (up_r, z)).start()
    remote(faces.at[1], faces.at[5], fx_send.at[1], fx_recv.at[1], (dn_r, z)).start()
    remote(faces.at[2, 0:8], faces.at[6, 0:8], fx_send.at[2], fx_recv.at[2], (r, up_z)).start()
    remote(faces.at[3, 0:8], faces.at[7, 0:8], fx_send.at[3], fx_recv.at[3], (r, dn_z)).start()

    def face_body(x, carry):
        remote(
            snap.at[:, x, NZL - 1, :], hz_lo.at[x], fx_send.at[4], fx_recv.at[4], (r, up_z)
        ).start()
        remote(snap.at[:, x, 0, :], hz_hi.at[x], fx_send.at[5], fx_recv.at[5], (r, dn_z)).start()
        return carry

    lax.fori_loop(0, NXL, face_body, 0)
    for zz in range(NZL):
        remote(
            snap.at[:, 0, zz, :], lay.at[NXL + 1, :, zsl(zz)], fx_send.at[6], fx_recv.at[6],
            (dn_r, z),
        ).start()
        remote(
            snap.at[:, NXL - 1, zz, :], lay.at[0, :, zsl(zz)], fx_send.at[7], fx_recv.at[7],
            (up_r, z),
        ).start()
    acc[...] = jnp.zeros_like(acc)
    acc2[...] = jnp.zeros_like(acc2)

    def gram_part(x):
        for zz in range(NZL):
            v = slab(x, zz)
            lay[x + 1, :, zsl(zz)] = v
            h, m, low = split3(v)
            f3[x, 0:64, zsl(zz)] = h
            f3[x, 64:128, zsl(zz)] = m
            f3[x, 128:192, zsl(zz)] = low
        acc[...] += nt_dot(f3[x, 0:128], f3[x])

    drain(fld.at[0], load_sem.at[0])
    gram_part(0)
    drain(fld.at[NXL - 1], load_sem.at[NXL - 1])

    gram_part(NXL - 1)

    def gram_body(x, carry):
        drain(fld.at[x], load_sem.at[x])
        gram_part(x)
        return carry

    lax.fori_loop(1, NXL - 1, gram_body, 0)

    def sum_rows(i, value):
        halves, diag = value
        for h in range(2):
            mine[i, h, 0:8] = halves[h]
            mine[i, h, 8:9] = diag
        for k in range(1, ROWS):
            to = (r + k) % ROWS
            remote(
                mine.at[i, to % 2], rows_buf.at[i, r], ar_send.at[2 * i], ar_recv.at[2 * i], (to, z)
            ).start()
        rows_buf[i, r] = mine[i, c]

    def sum_z(i):
        drain(rows_buf.at[i, 0 : ROWS - 1], ar_recv.at[2 * i])
        half[i] = tree_sum([rows_buf[i, k] for k in range(ROWS)])
        slot = c * HEIGHT + z
        for k in range(1, 2 * HEIGHT):
            to = (slot + k) % (2 * HEIGHT)
            remote(
                half.at[i], z_buf.at[i, slot], ar_send.at[2 * i + 1], ar_recv.at[2 * i + 1],
                (xy * 2 + to // HEIGHT, to % HEIGHT),
            ).start()
        z_buf[i, slot] = half[i]

    def sum_end(i):
        drain(z_buf.at[i, 0 : 2 * HEIGHT - 1], ar_recv.at[2 * i + 1])
        halves = [
            tree_sum([z_buf[i, h * HEIGHT + k, 0:8] for k in range(HEIGHT)]) for h in range(2)
        ]
        diag = tree_sum([z_buf[i, k, 8:9] for k in range(HEIGHT)])
        return unpack(halves, diag)

    a = acc[...]
    cross = a[0:64, 64:128] + a[0:64, 128:192]
    gram = (a[0:64, 0:64] + (cross + cross.T) + a[64:128, 64:128]) * (1.0 / CELLS)
    sum_rows(0, pack(gram))

    for i in range(4):
        drain(faces.at[4 + i] if i < 2 else faces.at[4 + i, 0:8], fx_recv.at[i])
    row_id = lax.broadcasted_iota(jnp.int32, (NZL, NY), 0)
    lane_id = lax.broadcasted_iota(jnp.int32, (NZL, NY), 1)
    ok_lo_x = jnp.where(r > 0, 1.0, 0.0).astype(F32)
    ok_hi_x = jnp.where(r < ROWS - 1, 1.0, 0.0).astype(F32)
    ok_lo_z = jnp.where(z > 0, 1.0, 0.0).astype(F32)
    ok_hi_z = jnp.where(z < HEIGHT - 1, 1.0, 0.0).astype(F32)
    for x in range(NXL):
        cc = cond[x]
        couple = lookup(mat[x], COUPLE_TABLE)
        half_c = 0.5 * cc
        diag = couple
        if x == 0:
            lo = 0.5 * (cc + faces[4]) * ok_lo_x
            diag = diag + half_c * (1.0 - ok_lo_x)
        else:
            lo = 0.5 * (cc + cond[x - 1])
        if x == NXL - 1:
            hi = 0.5 * (cc + faces[5]) * ok_hi_x
            diag = diag + half_c * (1.0 - ok_hi_x)
        else:
            hi = 0.5 * (cc + cond[x + 1])
        below = jnp.concatenate([faces[6, x : x + 1], cc[0 : NZL - 1]], axis=0)
        above = jnp.concatenate([cc[1:NZL], faces[7, x : x + 1]], axis=0)
        mask_lo = jnp.where(row_id == 0, ok_lo_z, 1.0)
        mask_hi = jnp.where(row_id == NZL - 1, ok_hi_z, 1.0)
        zlo = 0.5 * (cc + below) * mask_lo
        zhi = 0.5 * (cc + above) * mask_hi
        diag = diag + half_c * ((1.0 - mask_lo) + (1.0 - mask_hi))
        nxt = pltpu.roll(cc, NY - 1, 1)
        ly = jnp.where(lane_id == NY - 1, 0.0, 0.5 * (cc + nxt))
        edge = jnp.where((lane_id == 0) | (lane_id == NY - 1), half_c, 0.0)
        coef[0, x] = diag + edge
        coef[1, x] = lo
        coef[2, x] = hi
        coef[3, x] = zlo
        coef[4, x] = zhi
        coef[5, x] = ly


    def image(x, z0, z1, part):
        def at(xx, zz):
            return lay[xx, part, zsl(zz)]

        v = at(x + 1, z0)
        prev = hz_lo[x, part] if z0 == 0 else at(x + 1, z0 - 1)
        flux = coef[3, x, z0 : z0 + 1, :] * (prev - v)
        for zz in range(z0, z1):
            nxt = hz_hi[x, part] if zz == NZL - 1 else at(x + 1, zz + 1)

            def cf(i):
                return coef[i, x, zz : zz + 1, :]

            q = cf(5) * (v - pltpu.roll(v, NY - 1, 1))
            out = cf(0) * v - flux
            out += cf(1) * (v - at(x, zz))
            out += cf(2) * (v - at(x + 2, zz))
            flux = cf(4) * (v - nxt)
            out += flux + (q - pltpu.roll(q, 1, 1))
            for k, piece in enumerate(split3(out)):
                i3[x, k * M + part.start : k * M + part.stop, zsl(zz)] = piece
            v = nxt

    def images(x, z0, z1):
        for part in PARTS:
            image(x, z0, z1, part)

    def inner_body(x, carry):
        images(x, 1, NZL - 1)
        cells = slice(NY, LANES - NY)
        acc2[...] += nt_dot(f3[x, :, cells], i3[x, :, cells])
        return carry

    lax.fori_loop(1, NXL - 1, inner_body, 0)

    def outer():
        drain(hz_lo, fx_recv.at[4])
        drain(hz_hi, fx_recv.at[5])

        def end_body(i, carry):
            x = i * (NXL - 1)
            images(x, 0, NZL)
            acc2[...] += nt_dot(f3[x], i3[x])
            return carry

        def edge_image(x, carry):
            images(x, 0, 1)
            images(x, NZL - 1, NZL)
            return carry

        def edges(ref):
            return jnp.concatenate(
                [ref[x, :, zsl(zz)] for x in range(1, NXL - 1) for zz in (0, NZL - 1)], axis=1
            )

        lax.fori_loop(1, NXL - 1, edge_image, 0)
        acc2[...] += nt_dot(edges(f3), edges(i3))
        sum_z(0)
        drain(lay.at[NXL + 1], fx_recv.at[6])
        drain(lay.at[0], fx_recv.at[7])
        lax.fori_loop(0, 2, end_body, 0)

    outer()

    a = acc2[...]
    proj = (
        a[0:64, 0:64]
        + (a[0:64, 64:128] + a[64:128, 0:64])
        + (a[0:64, 128:192] + a[64:128, 64:128] + a[128:192, 0:64])
    ) * (1.0 / CELLS)
    sum_rows(1, pack(0.5 * (proj + proj.T)))
    g = sum_end(0)

    ri = lax.broadcasted_iota(jnp.int32, (M, M), 0)
    ci = lax.broadcasted_iota(jnp.int32, (M, M), 1)
    w = eliminate(jnp.concatenate([g, jnp.where(ri == ci, 1.0, 0.0).astype(F32)], axis=1))
    u = w[:, 0:M]
    d = jnp.sum(jnp.where(ri == ci, u, 0.0), axis=1, keepdims=True)
    rs = lax.rsqrt(d)
    linv = jnp.where(ci <= ri, w[:, M : 2 * M] * rs, 0.0)
    upper = jnp.where(ci >= ri, u * rs, 0.0)
    w_out[...] = jnp.concatenate([upper, linv], axis=1)
    h, m, low = split3(linv)
    zero = jnp.zeros_like(h)
    lst[0:64] = jnp.concatenate([h, h, h, m], axis=1)
    lst[64:128] = jnp.concatenate([low, m, zero, zero], axis=1)
    sum_z(1)

    step = 512

    def inverse_body(x, carry):
        for src, dst in ((f3, basis_v), (i3, applied_v)):
            out = dst.at[x].reshape(M * NZL, NY)
            for col in range(0, LANES, step):
                cells = slice(col, col + step)
                rhs = jnp.concatenate([src[x, :, cells], src[x, 0:64, cells]], axis=0)
                p = jnp.dot(lst[...], rhs, preferred_element_type=F32)
                p = p[0:64] + p[64:128]
                for k in range(step // NY):
                    out[pl.ds(col // NY + k, M, stride=NZL), :] = p[:, k * NY : (k + 1) * NY]
        return carry

    lax.fori_loop(0, NXL, inverse_body, 0)

    for i in range(4):
        drain(faces.at[4] if i < 2 else faces.at[4, 0:8], fx_send.at[i])
    drain(hz_lo, fx_send.at[4])
    drain(hz_hi, fx_send.at[5])
    drain(lay.at[0], fx_send.at[6])
    drain(lay.at[0], fx_send.at[7])
    for i in range(2):
        drain(rows_buf.at[i, 0 : ROWS - 1], ar_send.at[2 * i])
        drain(z_buf.at[i, 0 : 2 * HEIGHT - 1], ar_send.at[2 * i + 1])
    pt_out[...] = sum_end(1)


def last_kernel(basis_v, applied_v, w_in, pt, basis, applied, reduced, low_factor, sem):
    for x in range(NXL):
        pltpu.make_async_copy(basis_v.at[x], basis.at[:, x], sem).start()
    for x in range(NXL):
        pltpu.make_async_copy(applied_v.at[x], applied.at[:, x], sem).start()
    w = w_in[...]
    linv = w[:, M : 2 * M]
    low_factor[...] = w[:, 0:M].T
    hi = lax.Precision.HIGHEST
    t = jnp.dot(linv, pt[...], precision=hi, preferred_element_type=F32)
    reduced[...] = lax.dot_general(
        t, linv, (((1,), (1,)), ((), ())), precision=hi, preferred_element_type=F32
    )
    pltpu.make_async_copy(basis_v, basis_v, sem).wait()
    pltpu.make_async_copy(applied_v, applied_v, sem).wait()


def local(snapshots, material):
    any_ = pl.BlockSpec(memory_space=pl.ANY)
    vm = pl.BlockSpec(memory_space=pltpu.VMEM)
    dma, fbuf = pltpu.SemaphoreType.DMA, functools.partial(pltpu.VMEM, dtype=F32)
    wide = pltpu.VMEM((NXL, 192, LANES), BF16)
    held = fbuf((NXL, M, NZL, NY))
    basis_v, applied_v, w, pt = pl.pallas_call(
        first_kernel,
        out_shape=(held, held, fbuf((M, 2 * M)), fbuf((M, M))),
        in_specs=[any_, any_],
        out_specs=(vm, vm, vm, vm),
        scratch_shapes=[
            pltpu.VMEM((NXL, NZL, NY), jnp.int32),
            fbuf((NXL, M, NZL, NY)),
            fbuf((NXL + 2, M, LANES)),
            wide,
            wide,
            fbuf((NXL, M, NY)),
            fbuf((NXL, M, NY)),
            fbuf((NXL, NZL, NY)),
            fbuf((8, NZL, NY)),
            fbuf((6, NXL, NZL, NY)),
            fbuf((128, 192)),
            fbuf((192, 192)),
            fbuf((2, 2, 9, 128)),
            fbuf((2, ROWS, 9, 128)),
            fbuf((2, 2 * HEIGHT, 9, 128)),
            fbuf((2, 9, 128)),
            pltpu.VMEM((128, 256), BF16),
            dma((NXL + 1,)),
            dma((8,)),
            dma((8,)),
            dma((4,)),
            dma((4,)),
        ],
        compiler_params=pltpu.CompilerParams(
            collective_id=0, has_side_effects=True, vmem_limit_bytes=32 << 20
        ),
        name="gram_and_image",
    )(
        pltpu.with_memory_space_constraint(snapshots, pltpu.HBM),
        pltpu.with_memory_space_constraint(material, pltpu.HBM),
    )
    full = jax.ShapeDtypeStruct((M, NXL, NZL, NY), F32)
    small = jax.ShapeDtypeStruct((M, M), F32)
    return pl.pallas_call(
        last_kernel,
        out_shape=(full, full, small, small),
        in_specs=[vm, vm, vm, vm],
        out_specs=(any_, any_, vm, vm),
        scratch_shapes=[dma],
        compiler_params=pltpu.CompilerParams(vmem_limit_bytes=8 << 20),
        name="write_results",
    )(basis_v, applied_v, w, pt)


def solution(mesh):
    in_specs = (P(None, "rows", "height", None), P("rows", "height", None))
    out_specs = (P(None, "rows", "height", None), P(None, "rows", "height", None), P(), P())
    return jax.shard_map(local, mesh=mesh, in_specs=in_specs, out_specs=out_specs, check_vma=False)
```
